32 devices in a mesh: row: 8 (over z, x), col: 4 (over y, core).
Axes of the slice: x: 2, y: 2, z: 4, core: 2. Of those that a mesh axis runs over, the one named last changes fastest.
Arguments:
- blocks: float32 [2048, 4, 128, 128], P(('row', 'col')), may hold values from -0.25 to 0.25
- block_cols: int32 [2048, 4], P(('row', 'col')), may hold values from 0 to 255, as said below
- targets: float32 [32, 262144], P(None, ('row', 'col')), may hold values from -6 to 6
Outputs:
- solution: float32 [32, 32768], P(None, ('row', 'col'))
- residual: float32 [32, 262144], P(None, ('row', 'col'))
The draws below stay inside these ranges and needn't reach their ends.
Inputs may be any that keep to these rules, and one draw needn't show every extreme that they name: `block_cols`: the four indices of a block row differ. Block row i belongs to device d = i // 64, devices numbered row-major over (row, col); every index j of it satisfies (j // 8) % 4 == d % 4.
All inputs are finite; a program needn't handle non-finite values.
Results may differ from the reference program's by a relative error of at most 0.00012.
Values sent between devices are 32-bit elements; how exact they have to be, the bound alone decides.
No kernel may reach another device: no remote copies, remote signals or barrier semaphores. Data moves between devices by JAX's collectives and lax.ppermute only.
A program may use at most 128 MiB of HBM per device.

```python
import jax
import jax.numpy as jnp
from jax import lax

BS = 128
NRHS = 32
ITERS = 3
BRD = 64
CBD = 8
NBR = 2048
NBC = 256
ROWS = 262144
PARAMS = 32768
N_ROW = 8
N_COL = 4


def draw_block_cols(key, part):
    key = jax.random.fold_in(key, 5)
    first_key, second_key = jax.random.split(key)
    row_ids = jnp.arange(NBR, dtype=jnp.int32)
    col_group = row_ids // BRD % N_COL
    group_size = CBD * N_ROW
    quarter = group_size // 4
    base = jax.random.randint(first_key, (NBR, 1), 0, group_size, dtype=jnp.int32)
    offsets = jax.random.randint(second_key, (NBR, 4), 0, quarter, dtype=jnp.int32)
    local_ids = (base + jnp.arange(4, dtype=jnp.int32)[None, :] * quarter + offsets) % group_size
    result = (local_ids // CBD * N_COL + col_group[:, None]) * CBD + local_ids % CBD
    return result.astype(jnp.int32)


def level_of(rng, shape, cuts, smallest, largest):
    factor_of = 1.0
    for axis_at, blocks in cuts:
        heights = jax.random.uniform(jax.random.fold_in(jax.random.fold_in(rng, 6), axis_at), (blocks,), jnp.float32, smallest / len(cuts), largest / len(cuts))
        factor_of = factor_of * jnp.repeat(jnp.exp(heights), shape[axis_at] // blocks).reshape((-1,) + (1,) * (len(shape) - 1 - axis_at))
    return factor_of


def bell_draw(own_key, shape, deviation, reach, cuts=(), kind=jnp.bfloat16):
    level = level_of(own_key, shape, cuts, -0.22, 0.18) if cuts else 1.0
    values = jax.random.normal(own_key, shape, jnp.float32) * deviation * level
    return jnp.minimum(jnp.maximum(values, -reach), reach).astype(kind)


def setup_inputs(seed: int = 0) -> dict:
    arg_keys = jax.random.split(jax.random.key(seed), 4)
    return {
        "blocks": bell_draw(arg_keys[0], (NBR, 4, BS, BS), (4 * BS) ** -0.5, 0.25, ((0, 32),), jnp.float32),
        "block_cols": draw_block_cols(jax.random.fold_in(arg_keys[3], 71), 0),
        "targets": bell_draw(arg_keys[2], (NRHS, ROWS), 1.0, 6.0, ((1, 32),), jnp.float32),
    }


def chol_solve(matrix, right):
    lower_factor = jnp.linalg.cholesky(matrix)
    middle = lax.linalg.triangular_solve(lower_factor, right, left_side=True, lower=True)
    return lax.linalg.triangular_solve(lower_factor, middle, left_side=True, lower=True, transpose_a=True)

def apply_forward(blocks, block_cols, direction):
    rhs_count = direction.shape[0]
    tiles = direction.reshape(rhs_count, -1, BS)
    picked = jnp.take(tiles, block_cols.reshape(-1), axis=1)
    picked = picked.reshape(rhs_count, block_cols.shape[0], 4, BS)
    image = jnp.einsum('ikab,nikb->nia', blocks, picked, precision=lax.Precision.HIGHEST)
    return image.reshape(rhs_count, -1)

def apply_backward(blocks, block_cols, residual, segments):
    rhs_count = residual.shape[0]
    shaped = residual.reshape(rhs_count, blocks.shape[0], BS)
    pieces_all = jnp.einsum('ikab,nia->iknb', blocks, shaped, precision=lax.Precision.HIGHEST)
    pieces_all = pieces_all.reshape(-1, rhs_count, BS)
    summed = jax.ops.segment_sum(pieces_all, block_cols.reshape(-1), num_segments=segments)
    return summed.transpose(1, 0, 2).reshape(rhs_count, -1)

def gram_of(matrix):
    return jnp.dot(matrix.astype(jnp.float32), matrix.T.astype(jnp.float32), precision=lax.Precision.HIGHEST, preferred_element_type=jnp.float32)

def reference(blocks, block_cols, targets):
    residual = targets
    solution = jnp.zeros((NRHS, PARAMS), jnp.float32)
    gradient = apply_backward(blocks, block_cols, residual, NBC)
    grad_gram = gram_of(gradient)
    direction = gradient
    for iteration in range(ITERS):
        image = apply_forward(blocks, block_cols, direction)
        image_gram = gram_of(image)
        step_size = chol_solve(image_gram, grad_gram)
        solution = solution + jnp.dot(step_size.T, direction, precision=lax.Precision.HIGHEST)
        residual = residual - jnp.dot(step_size.T, image, precision=lax.Precision.HIGHEST)
        if iteration + 1 < ITERS:
            gradient = apply_backward(blocks, block_cols, residual, NBC)
            new_gram = gram_of(gradient)
            mix = chol_solve(grad_gram, new_gram)
            direction = gradient + jnp.dot(mix.T, direction, precision=lax.Precision.HIGHEST)
            grad_gram = new_gram
    return (solution, residual)
```

```python
import functools

import jax
import jax.numpy as jnp
from jax import lax
from jax.experimental import pallas as pl
from jax.experimental.pallas import tpu as pltpu
from jax.sharding import PartitionSpec as P

CBD = 8
COPY_ROWS = 4
STEP_ROWS = 16
MIB = 1024 * 1024
F32 = jnp.float32
BF16 = jnp.bfloat16


def split(value):
    high = value.astype(BF16)
    return high, (value - high.astype(F32)).astype(BF16)


def stack(value):
    return jnp.concatenate(split(value), axis=0)


def dot_last(left, right):
    return lax.dot_general(left, right, (((1,), (1,)), ((), ())), preferred_element_type=F32)


def dot_first(left, right):
    return lax.dot_general(left, right, (((1,), (0,)), ((), ())), preferred_element_type=F32)


def dot_small(left, right, left_dim):
    return lax.dot_general(
        left,
        right,
        (((left_dim,), (0,)), ((), ())),
        precision=lax.Precision.HIGHEST,
        preferred_element_type=F32,
    )


def fold(product):
    rows, lanes = product.shape[0] // 2, product.shape[1] // 2
    return product[:rows, :lanes] + (
        product[:rows, lanes:] + product[rows:, :lanes] + product[rows:, lanes:]
    )


def tile_at(index, tile):
    return pl.ds(pl.multiple_of(index * tile, tile), tile)


def backward_piece(cols_ref, row, weights, parts, sums_ref):
    rhs = parts.shape[0] // 2
    tile = parts.shape[1]
    product = dot_first(jnp.concatenate([parts, parts], axis=1), weights)
    product = product[:rhs] + product[rhs:]
    for k in range(4):
        at = cols_ref[row * 4 + k]
        sums_ref[at] = sums_ref[at] + product[:, k * tile : (k + 1) * tile]


def forward_piece(cols_ref, row, weights, halves_ref):
    picked = jnp.concatenate([halves_ref[cols_ref[row * 4 + k]] for k in range(4)], axis=1)
    return fold(dot_last(picked, weights))


def combine(coefficient_parts, high, low):
    rows = coefficient_parts.shape[0] // 2
    product = dot_first(coefficient_parts, high)
    return product[:rows] + (product[rows:] + dot_first(coefficient_parts[:rows], low))


def fill_halves(vector_refs, halves_ref):
    base = 0
    for vector_ref in vector_refs:

        @pl.loop(0, vector_ref.shape[0], unroll=CBD)
        def _(j):
            halves_ref[base + j] = stack(vector_ref[j])

        base += vector_ref.shape[0]


def empty_sums(sums_ref):
    @pl.loop(0, sums_ref.shape[0], unroll=CBD)
    def _(j):
        sums_ref[j] = jnp.zeros(sums_ref.shape[1:], F32)


def hand_out(sums_ref, share_refs, grams=None):
    size = CBD + int(grams is not None)
    slot = 0
    for share_ref in share_refs:
        for part in range(share_ref.shape[0] // size):

            @pl.loop(0, CBD, unroll=CBD)
            def _(j):
                share_ref[part * size + j] = sums_ref[slot * CBD + j]

            if grams is not None:
                share_ref[part * size + CBD] = grams
            slot += 1


def prepare_kernel(cols_ref, blocks_ref, source_ref, weights_ref, *refs):
    share_refs, (staged_ref, value_ref, sums_ref, semaphores) = refs[:-4], refs[-4:]
    chunks = blocks_ref.shape[0] // COPY_ROWS
    tile = blocks_ref.shape[-1]

    def copy(chunk):
        rows = pl.ds(chunk * COPY_ROWS, COPY_ROWS)
        return pltpu.make_async_copy(
            blocks_ref.at[rows], staged_ref.at[rows], semaphores.at[chunk]
        )

    value_copy = pltpu.make_async_copy(source_ref, value_ref, semaphores.at[chunks])
    value_copy.start()

    @pl.loop(0, chunks)
    def _(chunk):
        copy(chunk).start()

    empty_sums(sums_ref)
    value_copy.wait()

    @pl.loop(0, chunks, step=2)
    def _(chunk):
        copy(chunk).wait()
        copy(chunk + 1).wait()
        for i in range(2 * COPY_ROWS):
            row = chunk * COPY_ROWS + i
            wide = jnp.concatenate([staged_ref[row, k] for k in range(4)], axis=1)
            weights = stack(wide)
            weights_ref[row] = weights
            backward_piece(cols_ref, row, weights, stack(value_ref[:, tile_at(row, tile)]), sums_ref)

    hand_out(sums_ref, share_refs)


def prepare(cols, blocks, value, groups):
    block_rows, _, tile, _ = blocks.shape
    rhs = value.shape[0]
    shares = [jax.ShapeDtypeStruct((count * CBD, rhs, tile), F32) for count in groups]
    vmem = pl.BlockSpec(memory_space=pltpu.VMEM)
    return pl.pallas_call(
        prepare_kernel,
        in_specs=[
            pl.BlockSpec(memory_space=pltpu.SMEM),
            pl.BlockSpec(memory_space=pl.ANY),
            pl.BlockSpec(memory_space=pl.ANY),
        ],
        out_specs=[vmem] * (1 + len(groups)),
        out_shape=[pltpu.VMEM((block_rows, 2 * tile, 4 * tile), BF16)] + shares,
        scratch_shapes=[
            pltpu.VMEM(blocks.shape, F32),
            pltpu.VMEM(value.shape, F32),
            pltpu.VMEM((sum(groups) * CBD, rhs, tile), F32),
            pltpu.SemaphoreType.DMA((block_rows // COPY_ROWS + 1,)),
        ],
        compiler_params=pltpu.CompilerParams(vmem_limit_bytes=24 * MIB),
        cost_estimate=pl.CostEstimate(
            flops=6 * blocks.size * rhs, bytes_accessed=blocks.size * 4, transcendentals=0
        ),
    )(
        cols,
        pltpu.with_memory_space_constraint(blocks, pltpu.HBM),
        pltpu.with_memory_space_constraint(value, pltpu.HBM),
    )


def sweep_kernel(inputs, outputs, mode, cols_ref, weights_ref, *refs):
    first, backward = mode == "first", mode != "last"
    vector_refs, refs = refs[:inputs], refs[inputs:]
    share_ref, refs = refs[0], refs[1:]
    if not first:
        base_ref, coefficient_ref, old_ref, refs = refs[0], refs[1], refs[2], refs[3:]
    image_ref, refs = refs[0], refs[1:]
    raw_ref = image_ref
    if mode == "middle":
        raw_ref, refs = refs[0], refs[1:]
    if backward:
        sum_refs, refs = refs[:outputs], refs[outputs:]
        sums_ref, refs = refs[0], refs[1:]
    else:
        gram_ref, refs = refs[0], refs[1:]
    halves_ref, parts_ref, products_ref = refs
    share, rhs, tile = share_ref.shape
    chunks = weights_ref.shape[0] // STEP_ROWS

    fill_halves(vector_refs, halves_ref)
    if backward:
        empty_sums(sums_ref)
    products_ref[...] = jnp.zeros_like(products_ref)
    if not first:
        coefficient_parts = stack(coefficient_ref[...].T)

    def ahead(chunk):
        for i in range(STEP_ROWS):
            row = chunk * STEP_ROWS + i
            value = forward_piece(cols_ref, row, weights_ref[row], halves_ref)
            if backward:
                raw_ref[:, tile_at(row, tile)] = value
            parts_ref[lax.rem(chunk, 2), :, i * tile : (i + 1) * tile] = stack(value)

    def behind(chunk):
        parts = parts_ref[lax.rem(chunk, 2)]
        at = tile_at(chunk, STEP_ROWS * tile)
        if first:
            left = right = parts
        else:
            image = base_ref[:, at] + combine(coefficient_parts, parts[:rhs], parts[rhs:])
            image_ref[:, at] = image
            right = stack(image)
            left = jnp.concatenate([right, stack(old_ref[:, at])], axis=0)
        products_ref[...] += dot_last(left, right)
        if backward:
            for i in range(STEP_ROWS):
                row = chunk * STEP_ROWS + i
                backward_piece(
                    cols_ref, row, weights_ref[row], parts[:, i * tile : (i + 1) * tile], sums_ref
                )

    ahead(0)

    @pl.loop(1, chunks)
    def _(chunk):
        ahead(chunk)
        behind(chunk - 1)

    behind(chunks - 1)
    own = jnp.concatenate([stack(share_ref[j]) for j in range(share)], axis=1)
    grams = [fold(dot_last(own, own)), fold(products_ref[: 2 * rhs])]
    if not first:
        grams.append(fold(products_ref[2 * rhs :]))
    grams.append(jnp.zeros((rhs, tile - len(grams) * rhs), F32))
    grams = jnp.concatenate(grams, axis=1)
    if backward:
        hand_out(sums_ref, sum_refs, grams)
    else:
        gram_ref[...] = grams


def sweep(cols, weights, vectors, groups, share, mode, extra=()):
    block_rows, _, width = weights.shape
    slots = sum(groups)
    _, rhs, tile = share.shape
    grams = 2 if mode == "first" else 3
    vmem = pl.BlockSpec(memory_space=pltpu.VMEM)
    wide = jax.ShapeDtypeStruct((rhs, block_rows * tile), F32)
    out_shape = [wide]
    scratch = [
        pltpu.VMEM((slots * CBD, 2 * rhs, tile), BF16),
        pltpu.VMEM((2, 2 * rhs, STEP_ROWS * tile), BF16),
        pltpu.VMEM(((grams - 1) * 2 * rhs, 2 * rhs), F32),
    ]
    if mode == "middle":
        out_shape.append(wide)
    if mode != "last":
        out_shape += [
            jax.ShapeDtypeStruct((count * (CBD + 1), rhs, tile), F32) for count in groups
        ]
        scratch = [pltpu.VMEM((slots * CBD, rhs, tile), F32)] + scratch
    else:
        out_shape.append(jax.ShapeDtypeStruct((rhs, tile), F32))
    operands = list(vectors) + [share] + list(extra)
    return pl.pallas_call(
        functools.partial(sweep_kernel, len(vectors), len(groups), mode),
        in_specs=[pl.BlockSpec(memory_space=pltpu.SMEM)] + [vmem] * (1 + len(operands)),
        out_specs=[vmem] * len(out_shape),
        out_shape=out_shape,
        scratch_shapes=scratch,
        compiler_params=pltpu.CompilerParams(vmem_limit_bytes=14 * MIB),
        cost_estimate=pl.CostEstimate(
            flops=6 * (1 + int(mode != "last")) * weights.size * rhs // 2,
            bytes_accessed=weights.size,
            transcendentals=0,
        ),
    )(cols, pltpu.with_memory_space_constraint(weights, pltpu.VMEM), *operands)


def eliminate(systems):
    size = systems[0][0].shape[0]
    row_ids = lax.broadcasted_iota(jnp.int32, (size, 1), 0)
    wides = [jnp.concatenate(pair, axis=1) for pair in systems]
    for k in range(0, size, 2):
        done = []
        for wide in wides:
            first = jnp.broadcast_to(wide[:, k : k + 1], wide.shape)
            second = jnp.broadcast_to(wide[:, k + 1 : k + 2], wide.shape)
            a, c = first[k : k + 1], first[k + 1 : k + 2]
            b, d = second[k : k + 1], second[k + 1 : k + 2]
            one, two = wide[k : k + 1], wide[k + 1 : k + 2]
            inverse = 1.0 / (a * d - b * c)
            top = (d * one - b * two) * inverse
            low = (a * two - c * one) * inverse
            rest = wide - first * top - second * low
            done.append(jnp.where(row_ids == k, top, jnp.where(row_ids == k + 1, low, rest)))
        wides = done
    return [wide[:, size:] for wide in wides]


def identity(size):
    rows = lax.broadcasted_iota(jnp.int32, (size, size), 0)
    lanes = lax.broadcasted_iota(jnp.int32, (size, size), 1)
    return jnp.where(rows == lanes, 1.0, 0.0).astype(F32)


def coefficients(grams, previous):
    rhs = grams.shape[0]
    own_gram = grams[:, :rhs]
    image_gram = grams[:, rhs : 2 * rhs]
    if previous is None:
        return own_gram, image_gram, None
    old_inverse, old_gram = previous
    cross = grams[:, 2 * rhs : 3 * rhs]
    mix = dot_small(old_inverse, own_gram, 1)
    image_gram = image_gram + (
        dot_small(mix, cross, 0)
        + dot_small(cross, mix, 0)
        + dot_small(mix, dot_small(old_gram, mix, 1), 0)
    )
    return own_gram, image_gram, mix


def added(refs):
    total = refs[0][...]
    for ref in refs[1:]:
        total = total + ref[...]
    return total


def first_steps_kernel(*refs):
    step_ref, inverse_ref, gram_ref, minus_ref = refs[-4:]
    own_gram, image_gram, _ = coefficients(added(refs[:-4]), None)
    step, inverse = eliminate([(image_gram, own_gram), (own_gram, identity(own_gram.shape[0]))])
    step_ref[...] = step
    inverse_ref[...] = inverse
    gram_ref[...] = image_gram
    minus_ref[...] = -step


def next_steps_kernel(*refs):
    old_step_ref, old_inverse_ref, old_gram_ref = refs[-9:-6]
    step_ref, inverse_ref, gram_ref, mix_ref, base_ref, raw_ref = refs[-6:]
    previous = (old_inverse_ref[...], old_gram_ref[...])
    own_gram, image_gram, mix = coefficients(added(refs[:-9]), previous)
    step, inverse = eliminate([(image_gram, own_gram), (own_gram, identity(own_gram.shape[0]))])
    step_ref[...] = step
    inverse_ref[...] = inverse
    gram_ref[...] = image_gram
    mix_ref[...] = mix
    base_ref[...] = -step - dot_small(mix, step, 1)
    raw_ref[...] = dot_small(old_step_ref[...], step, 1)


def cost(flops, elements):
    return pl.CostEstimate(flops=flops, bytes_accessed=4 * elements, transcendentals=0)


def small_call(kernel, count, *operands):
    rhs = operands[0].shape[0]
    return pl.pallas_call(
        kernel,
        out_shape=[jax.ShapeDtypeStruct((rhs, rhs), F32)] * count,
        compiler_params=pltpu.CompilerParams(vmem_limit_bytes=2 * MIB),
        cost_estimate=cost(4 * 10**9, MIB),
    )(*operands)


def whole(ref):
    return jnp.concatenate([ref[j] for j in range(ref.shape[0])], axis=1)


def place(ref, value):
    tile = ref.shape[2]
    for j in range(ref.shape[0]):
        ref[j] = value[:, j * tile : (j + 1) * tile]


def gradient_kernel(g1_ref, q0_ref, p0_ref, step0_ref, step1_ref, mix_ref, g2_ref):
    q0 = whole(q0_ref)
    normal = q0 - dot_small(step0_ref[...], whole(p0_ref), 0) + dot_small(mix_ref[...], q0, 0)
    place(g2_ref, whole(g1_ref) - dot_small(step1_ref[...], normal, 0))


def next_gradient(*operands):
    return pl.pallas_call(
        gradient_kernel,
        out_shape=jax.ShapeDtypeStruct(operands[0].shape, F32),
        compiler_params=pltpu.CompilerParams(vmem_limit_bytes=4 * MIB),
        cost_estimate=cost(10**9, MIB),
    )(*operands)


def solution_kernel(g0_ref, g1_ref, step0_ref, step1_ref, mix_ref, direction_ref, sol_ref):
    g0 = whole(g0_ref)
    direction = whole(g1_ref) + dot_small(mix_ref[...], g0, 0)
    place(direction_ref, direction)
    sol_ref[...] = dot_small(step0_ref[...], g0, 0) + dot_small(step1_ref[...], direction, 0)


def solution_so_far(g0, *operands):
    row = jax.ShapeDtypeStruct((g0.shape[1], g0.shape[0] * g0.shape[2]), F32)
    return pl.pallas_call(
        solution_kernel,
        out_shape=[jax.ShapeDtypeStruct(g0.shape, F32), row],
        compiler_params=pltpu.CompilerParams(vmem_limit_bytes=4 * MIB),
        cost_estimate=cost(10**9, MIB),
    )(g0, *operands)


def images_kernel(y0_ref, y1_ref, u0_ref, mix_ref, base_ref, image_ref, next_ref):
    of_y0 = stack(mix_ref[...].T)
    of_u0 = stack(base_ref[...].T)
    width = 1024

    @pl.loop(0, y0_ref.shape[1] // width)
    def _(i):
        at = tile_at(i, width)
        y1 = y1_ref[:, at]
        image_ref[:, at] = y1 + combine(of_y0, *split(y0_ref[:, at]))
        next_ref[:, at] = y1 + combine(of_u0, *split(u0_ref[:, at]))


def images(y0, *operands):
    return pl.pallas_call(
        images_kernel,
        out_shape=[jax.ShapeDtypeStruct(y0.shape, F32)] * 2,
        compiler_params=pltpu.CompilerParams(vmem_limit_bytes=12 * MIB),
        cost_estimate=cost(3 * 10**9, MIB),
    )(y0, *operands)


def residual_kernel(y0_ref, image_ref, targets_ref, step0_ref, step1_ref, resid_ref):
    parts = stack(-jnp.concatenate([step0_ref[...], step1_ref[...]], axis=0).T)
    width = 1024

    @pl.loop(0, y0_ref.shape[1] // width)
    def _(i):
        at = tile_at(i, width)
        pair = jnp.concatenate([y0_ref[:, at], image_ref[:, at]], axis=0)
        resid_ref[:, at] = targets_ref[:, at] + combine(parts, *split(pair))


def residual_so_far(y0, *operands):
    return pl.pallas_call(
        residual_kernel,
        out_shape=jax.ShapeDtypeStruct(y0.shape, F32),
        compiler_params=pltpu.CompilerParams(vmem_limit_bytes=12 * MIB),
        cost_estimate=cost(2 * 10**9, 2 * MIB),
    )(y0, *operands)


def finish_kernel(*refs):
    *gram_refs, inverse_ref, gram_ref, resid_ref, image_ref, old_image_ref = refs[:-7]
    share_ref, old_ref, sol_ref, out_sol_ref, out_ref, new_ref, semaphores = refs[-7:]
    previous = (inverse_ref[...], gram_ref[...])
    own_gram, image_gram, mix = coefficients(added(gram_refs), previous)
    (step,) = eliminate([(image_gram, own_gram)])
    tile = share_ref.shape[2]
    both = jnp.concatenate([step, dot_small(mix, step, 1)], axis=0)
    pairs = [jnp.concatenate([share_ref[j], old_ref[j]], axis=0) for j in range(share_ref.shape[0])]
    out_sol_ref[...] = sol_ref[...] + dot_small(both, jnp.concatenate(pairs, axis=1), 0)
    minus = stack(-both.T)
    width = resid_ref.shape[1] // semaphores.shape[0]
    copies = []
    for i in range(semaphores.shape[0]):
        at = slice(i * width, (i + 1) * width)
        pair = jnp.concatenate([image_ref[:, at], old_image_ref[:, at]], axis=0)
        new_ref[:, at] = resid_ref[:, at] + combine(minus, *split(pair))
        copies.append(
            pltpu.make_async_copy(new_ref.at[:, at], out_ref.at[:, at], semaphores.at[i])
        )
        copies[-1].start()
    for copy in copies:
        copy.wait()


def finish(grams, previous, resid, image, old_image, share, old_share, sol):
    vmem = pl.BlockSpec(memory_space=pltpu.VMEM)
    return pl.pallas_call(
        finish_kernel,
        in_specs=[vmem] * (len(grams) + len(previous) + 6),
        out_specs=[vmem, pl.BlockSpec(memory_space=pl.ANY)],
        scratch_shapes=[pltpu.VMEM(resid.shape, F32), pltpu.SemaphoreType.DMA((4,))],
        out_shape=[
            jax.ShapeDtypeStruct(sol.shape, F32),
            jax.ShapeDtypeStruct(resid.shape, F32),
        ],
        compiler_params=pltpu.CompilerParams(vmem_limit_bytes=12 * MIB),
    )(*grams, *previous, resid, image, old_image, share, old_share, sol)


def mixed(small, wide):
    return jnp.einsum("mn,jmb->jnb", small, wide, precision=lax.Precision.HIGHEST)


def sum_kernel(starts, *refs):
    parts, outs = refs[: len(starts)], refs[len(starts) :]
    size = outs[0].shape[0] + len(outs) - 1
    total = parts[0][starts[0] : starts[0] + size]
    for start, part in zip(starts[1:], parts[1:]):
        total = total + part[start : start + size]
    if len(outs) == 1:
        outs[0][...] = total
    else:
        outs[0][...] = total[: size - 1]
        outs[1][...] = total[size - 1]


def sum_of(parts, size, apart=False):
    rest = parts[0][0].shape[1:]
    if apart:
        out_shape = [jax.ShapeDtypeStruct((size - 1,) + rest, F32), jax.ShapeDtypeStruct(rest, F32)]
    else:
        out_shape = [jax.ShapeDtypeStruct((size,) + rest, F32)]
    out = pl.pallas_call(
        functools.partial(sum_kernel, [start for _, start in parts]),
        out_shape=out_shape,
        compiler_params=pltpu.CompilerParams(vmem_limit_bytes=4 * MIB),
    )(*[array for array, _ in parts])
    return out if apart else out[0]


def sum_whole(parts):
    return sum_of([(part, 0) for part in parts], parts[0].shape[0])


def join_kernel(*refs):
    size = refs[0].shape[0]
    for i, part in enumerate(refs[: refs[-1].shape[0] // size]):
        refs[-1][i * size : (i + 1) * size] = part[...]


def join(parts, after):
    shape = parts[0].shape
    vmem = pl.BlockSpec(memory_space=pltpu.VMEM)
    return pl.pallas_call(
        join_kernel,
        in_specs=[vmem] * len(parts) + [pl.BlockSpec(memory_space=pl.ANY)] * len(after),
        out_specs=vmem,
        out_shape=jax.ShapeDtypeStruct((len(parts) * shape[0],) + shape[1:], F32),
        compiler_params=pltpu.CompilerParams(vmem_limit_bytes=4 * MIB),
    )(*parts, *after)


class Ring:
    def __init__(self, count):
        self.nz = 4 if count % 4 == 0 else count
        self.nx = count // self.nz
        self.order = [0] + list(range(1, self.nz, 2)) + list(range(2, self.nz, 2))[::-1]

    def row(self, place, x):
        return self.order[place % self.nz] * self.nx + x % self.nx

    def next_z(self, value, by=1):
        pairs = [
            (self.row(p, x), self.row(p + by, x)) for p in range(self.nz) for x in range(self.nx)
        ]
        return lax.ppermute(value, "row", pairs)

    def next_x(self, value):
        pairs = [
            (self.row(p, x), self.row(p, x + 1)) for p in range(self.nz) for x in range(self.nx)
        ]
        return lax.ppermute(value, "row", pairs)

    def place_of(self, row):
        z = row // self.nx
        return jnp.where(z % 2 == 1, (z + 1) // 2, (self.nz - z // 2) % self.nz)

    def slot_of(self, row):
        me = lax.axis_index("row")
        back_z = (self.place_of(me) - self.place_of(row) + self.nz) % self.nz
        back_x = (me % self.nx - row % self.nx + self.nx) % self.nx
        return back_z * self.nx + back_x

    def along_x(self, share):
        pieces = [share]
        for _ in range(1, self.nx):
            pieces.append(self.next_x(pieces[-1]))
        return pieces

    def gather(self, share, after=()):
        row = self.along_x(share)
        arrays = list(row)
        for _ in range(self.nz // 2):
            share = self.next_z(share)
            last = [share, arrays[-1], *after]
            arrays += self.along_x(share)
        back = []
        for _ in range((self.nz - 1) // 2):
            back.insert(0, self.next_z(back[0] if back else join(row, last), -1))
        return arrays + back

    def groups(self):
        back = (self.nz - 1) // 2
        return [1] * self.nx + [self.nx] * back + [1] * (self.nx * (self.nz - 1 - back))

    def scatter(self, arrays, apart=False):
        steps_back = (self.nz - 1) // 2
        size = arrays[0].shape[0]
        own, arrays = arrays[: self.nx], arrays[self.nx :]
        backs, arrays = arrays[:steps_back], arrays[steps_back:]

        def over_x(slots):
            parts = []
            for t in list(range(1, self.nx)) + [0]:
                if parts:
                    whole = len(parts) == 1 and parts[0][0].shape[0] == size
                    parts = [(self.next_x(parts[0][0] if whole else sum_of(parts, size)), 0)]
                parts = parts + slots[t]
            return parts

        ahead = []
        for f in range(self.nz // 2, 0, -1):
            at = (self.nz - f - 1 - steps_back) * self.nx
            piece = sum_of(over_x([[(arrays[at + t], 0)] for t in range(self.nx)]), size)
            ahead.append((self.next_z(piece, f), 0))
        back = [self.next_z(backs[s - 1], -s) for s in range(steps_back, 0, -1)]
        here = [
            [(own[t], 0)] + [(array, t * size) for array in back] for t in range(self.nx)
        ]
        return sum_of(over_x(here) + ahead, size, apart)


def exchanges(axes):
    steps = []
    for axis in axes:
        bits = (lax.axis_size(axis) - 1).bit_length()
        while bits:
            taken = 2 if bits > 1 else 1
            bits -= taken
            steps.append((axis, [flip << bits for flip in range(1, 1 << taken)]))
    return steps


def sum_over(value, axes):
    parts = [value]
    for at, (axis, flips) in enumerate(exchanges(axes)):
        if at:
            value = sum_whole(parts)
        parts = [value]
        for flip in flips:
            pairs = [(i, i ^ flip) for i in range(lax.axis_size(axis))]
            parts.append(lax.ppermute(value, axis, pairs))
    return parts


def body(blocks, block_cols, targets):
    row_count = lax.axis_size("row")
    col_count = lax.axis_size("col")
    ring = Ring(row_count)
    owner = block_cols // CBD // col_count
    cols = (ring.slot_of(owner) * CBD + block_cols % CBD).reshape(-1)

    groups = ring.groups()
    weights, *sums = prepare(cols, blocks, targets, groups)
    g0 = ring.scatter(sums)

    y0, *sums = sweep(cols, weights, ring.gather(g0), groups, g0, "first")
    q0, grams = ring.scatter(sums, True)
    grams = sum_over(grams, ("col",))
    step0, inverse, image_gram, minus = small_call(first_steps_kernel, 4, *grams)

    g1 = g0 + mixed(minus, q0)
    y1, u0, *sums = sweep(
        cols, weights, ring.gather(q0, [step0]), groups, g1, "middle", (y0, minus, y0)
    )
    p0, grams = ring.scatter(sums, True)
    grams = sum_over(grams, ("col",))
    step1, inverse, image_gram, mix, of_u0, of_raw = small_call(
        next_steps_kernel, 6, *grams, step0, inverse, image_gram
    )

    g2 = next_gradient(g1, q0, p0, step0, step1, mix)
    image, base = images(y0, y1, u0, mix, of_u0)
    y2, grams = sweep(
        cols, weights, ring.gather(p0), groups, g2, "last", (base, of_raw, image)
    )
    grams = sum_over(grams, ("col", "row"))
    direction, solution = solution_so_far(g0, g1, step0, step1, mix)
    residual = residual_so_far(y0, image, targets, step0, step1)
    return finish(
        grams, (inverse, image_gram), residual, y2, image, g2, direction, solution
    )


def solution(mesh):
    placed = (P(("row", "col"), None, None, None), P(("row", "col"), None), P(None, ("row", "col")))
    return jax.shard_map(
        body,
        mesh=mesh,
        in_specs=placed,
        out_specs=(P(None, ("row", "col")), P(None, ("row", "col"))),
        check_vma=False,
    )
```

```python
import functools

import jax
import jax.numpy as jnp
from jax import lax
from jax.experimental import pallas as pl
from jax.experimental.pallas import tpu as pltpu
from jax.sharding import PartitionSpec as P

CBD = 8
COPY_ROWS = 4
STEP_ROWS = 32
MIB = 1024 * 1024
F32 = jnp.float32
BF16 = jnp.bfloat16


def split(value):
    high = value.astype(BF16)
    return high, (value - high.astype(F32)).astype(BF16)


def stack(value):
    return jnp.concatenate(split(value), axis=0)


def dot_last(left, right):
    return lax.dot_general(left, right, (((1,), (1,)), ((), ())), preferred_element_type=F32)


def dot_first(left, right):
    return lax.dot_general(left, right, (((1,), (0,)), ((), ())), preferred_element_type=F32)


def dot_small(left, right, left_dim):
    return lax.dot_general(
        left,
        right,
        (((left_dim,), (0,)), ((), ())),
        precision=lax.Precision.HIGHEST,
        preferred_element_type=F32,
    )


def fold(product):
    rows, lanes = product.shape[0] // 2, product.shape[1] // 2
    return product[:rows, :lanes] + (
        product[:rows, lanes:] + product[rows:, :lanes] + product[rows:, lanes:]
    )


def tile_at(index, tile):
    return pl.ds(pl.multiple_of(index * tile, tile), tile)


def backward_piece(cols_ref, row, weights, parts, sums_ref):
    rhs = parts.shape[0] // 2
    tile = parts.shape[1]
    product = dot_first(jnp.concatenate([parts, parts], axis=1), weights)
    product = product[:rhs] + product[rhs:]
    for k in range(4):
        at = cols_ref[row * 4 + k]
        sums_ref[at] = sums_ref[at] + product[:, k * tile : (k + 1) * tile]


def forward_piece(cols_ref, row, weights, halves_ref):
    picked = jnp.concatenate([halves_ref[cols_ref[row * 4 + k]] for k in range(4)], axis=1)
    return fold(dot_last(picked, weights))


def combine(coefficient_parts, high, low):
    rows = coefficient_parts.shape[0] // 2
    product = dot_first(coefficient_parts, high)
    return product[:rows] + (product[rows:] + dot_first(coefficient_parts[:rows], low))


def fill_halves(vector_refs, halves_ref):
    base = 0
    for vector_ref in vector_refs:

        @pl.loop(0, vector_ref.shape[0], unroll=CBD)
        def _(j):
            halves_ref[base + j] = stack(vector_ref[j])

        base += vector_ref.shape[0]


def empty_sums(sums_ref):
    @pl.loop(0, sums_ref.shape[0], unroll=CBD)
    def _(j):
        sums_ref[j] = jnp.zeros(sums_ref.shape[1:], F32)


def hand_out(sums_ref, share_refs, grams=None):
    size = CBD + int(grams is not None)
    slot = 0
    for share_ref in share_refs:
        for part in range(share_ref.shape[0] // size):

            @pl.loop(0, CBD, unroll=CBD)
            def _(j):
                share_ref[part * size + j] = sums_ref[slot * CBD + j]

            if grams is not None:
                share_ref[part * size + CBD] = grams
            slot += 1


def prepare_kernel(cols_ref, blocks_ref, source_ref, weights_ref, *refs):
    share_refs, (staged_ref, value_ref, sums_ref, semaphores) = refs[:-4], refs[-4:]
    chunks = blocks_ref.shape[0] // COPY_ROWS
    tile = blocks_ref.shape[-1]

    def copy(chunk):
        rows = pl.ds(chunk * COPY_ROWS, COPY_ROWS)
        return pltpu.make_async_copy(
            blocks_ref.at[rows], staged_ref.at[rows], semaphores.at[chunk]
        )

    value_copy = pltpu.make_async_copy(source_ref, value_ref, semaphores.at[chunks])
    value_copy.start()

    @pl.loop(0, chunks)
    def _(chunk):
        copy(chunk).start()

    empty_sums(sums_ref)
    value_copy.wait()

    @pl.loop(0, chunks, step=2)
    def _(chunk):
        copy(chunk).wait()
        copy(chunk + 1).wait()
        for i in range(2 * COPY_ROWS):
            row = chunk * COPY_ROWS + i
            wide = jnp.concatenate([staged_ref[row, k] for k in range(4)], axis=1)
            weights = stack(wide)
            weights_ref[row] = weights
            backward_piece(cols_ref, row, weights, stack(value_ref[:, tile_at(row, tile)]), sums_ref)

    hand_out(sums_ref, share_refs)


def prepare(cols, blocks, value, groups):
    block_rows, _, tile, _ = blocks.shape
    rhs = value.shape[0]
    shares = [jax.ShapeDtypeStruct((count * CBD, rhs, tile), F32) for count in groups]
    vmem = pl.BlockSpec(memory_space=pltpu.VMEM)
    return pl.pallas_call(
        prepare_kernel,
        in_specs=[
            pl.BlockSpec(memory_space=pltpu.SMEM),
            pl.BlockSpec(memory_space=pl.ANY),
            pl.BlockSpec(memory_space=pl.ANY),
        ],
        out_specs=[vmem] * (1 + len(groups)),
        out_shape=[pltpu.VMEM((block_rows, 2 * tile, 4 * tile), BF16)] + shares,
        scratch_shapes=[
            pltpu.VMEM(blocks.shape, F32),
            pltpu.VMEM(value.shape, F32),
            pltpu.VMEM((sum(groups) * CBD, rhs, tile), F32),
            pltpu.SemaphoreType.DMA((block_rows // COPY_ROWS + 1,)),
        ],
        compiler_params=pltpu.CompilerParams(vmem_limit_bytes=24 * MIB),
        cost_estimate=pl.CostEstimate(
            flops=6 * blocks.size * rhs, bytes_accessed=blocks.size * 4, transcendentals=0
        ),
    )(
        cols,
        pltpu.with_memory_space_constraint(blocks, pltpu.HBM),
        pltpu.with_memory_space_constraint(value, pltpu.HBM),
    )


def sweep_kernel(inputs, outputs, mode, cols_ref, weights_ref, *refs):
    first, backward = mode == "first", mode != "last"
    vector_refs, refs = refs[:inputs], refs[inputs:]
    share_ref, refs = refs[0], refs[1:]
    if not first:
        base_ref, coefficient_ref, old_ref, refs = refs[0], refs[1], refs[2], refs[3:]
    image_ref, refs = refs[0], refs[1:]
    raw_ref = image_ref
    if mode == "middle":
        raw_ref, refs = refs[0], refs[1:]
    if backward:
        sum_refs, refs = refs[:outputs], refs[outputs:]
        sums_ref, refs = refs[0], refs[1:]
    else:
        gram_ref, refs = refs[0], refs[1:]
    halves_ref, parts_ref, products_ref = refs
    share, rhs, tile = share_ref.shape
    chunks = weights_ref.shape[0] // STEP_ROWS

    fill_halves(vector_refs, halves_ref)
    if backward:
        empty_sums(sums_ref)
    products_ref[...] = jnp.zeros_like(products_ref)
    if not first:
        coefficient_parts = stack(coefficient_ref[...].T)

    def ahead(chunk):
        for i in range(STEP_ROWS):
            row = chunk * STEP_ROWS + i
            value = forward_piece(cols_ref, row, weights_ref[row], halves_ref)
            if backward:
                raw_ref[:, tile_at(row, tile)] = value
            parts_ref[lax.rem(chunk, 2), :, i * tile : (i + 1) * tile] = stack(value)

    def behind(chunk):
        parts = parts_ref[lax.rem(chunk, 2)]
        at = tile_at(chunk, STEP_ROWS * tile)
        if first:
            left = right = parts
        else:
            image = base_ref[:, at] + combine(coefficient_parts, parts[:rhs], parts[rhs:])
            image_ref[:, at] = image
            right = stack(image)
            left = jnp.concatenate([right, stack(old_ref[:, at])], axis=0)
        products_ref[...] += dot_last(left, right)
        if backward:
            for i in range(STEP_ROWS):
                row = chunk * STEP_ROWS + i
                backward_piece(
                    cols_ref, row, weights_ref[row], parts[:, i * tile : (i + 1) * tile], sums_ref
                )

    ahead(0)

    @pl.loop(1, chunks)
    def _(chunk):
        ahead(chunk)
        behind(chunk - 1)

    behind(chunks - 1)
    own = jnp.concatenate([stack(share_ref[j]) for j in range(share)], axis=1)
    grams = [fold(dot_last(own, own)), fold(products_ref[: 2 * rhs])]
    if not first:
        grams.append(fold(products_ref[2 * rhs :]))
    grams.append(jnp.zeros((rhs, tile - len(grams) * rhs), F32))
    grams = jnp.concatenate(grams, axis=1)
    if backward:
        hand_out(sums_ref, sum_refs, grams)
    else:
        gram_ref[...] = grams


def sweep(cols, weights, vectors, groups, share, mode, extra=()):
    block_rows, _, width = weights.shape
    slots = sum(groups)
    _, rhs, tile = share.shape
    grams = 2 if mode == "first" else 3
    vmem = pl.BlockSpec(memory_space=pltpu.VMEM)
    wide = jax.ShapeDtypeStruct((rhs, block_rows * tile), F32)
    out_shape = [wide]
    scratch = [
        pltpu.VMEM((slots * CBD, 2 * rhs, tile), BF16),
        pltpu.VMEM((2, 2 * rhs, STEP_ROWS * tile), BF16),
        pltpu.VMEM(((grams - 1) * 2 * rhs, 2 * rhs), F32),
    ]
    if mode == "middle":
        out_shape.append(wide)
    if mode != "last":
        out_shape += [
            jax.ShapeDtypeStruct((count * (CBD + 1), rhs, tile), F32) for count in groups
        ]
        scratch = [pltpu.VMEM((slots * CBD, rhs, tile), F32)] + scratch
    else:
        out_shape.append(jax.ShapeDtypeStruct((rhs, tile), F32))
    operands = list(vectors) + [share] + list(extra)
    return pl.pallas_call(
        functools.partial(sweep_kernel, len(vectors), len(groups), mode),
        in_specs=[pl.BlockSpec(memory_space=pltpu.SMEM)] + [vmem] * (1 + len(operands)),
        out_specs=[vmem] * len(out_shape),
        out_shape=out_shape,
        scratch_shapes=scratch,
        compiler_params=pltpu.CompilerParams(vmem_limit_bytes=14 * MIB),
        cost_estimate=pl.CostEstimate(
            flops=6 * (1 + int(mode != "last")) * weights.size * rhs // 2,
            bytes_accessed=weights.size,
            transcendentals=0,
        ),
    )(cols, pltpu.with_memory_space_constraint(weights, pltpu.VMEM), *operands)


def eliminate(systems):
    size = systems[0][0].shape[0]
    row_ids = lax.broadcasted_iota(jnp.int32, (size, 1), 0)
    wides = [jnp.concatenate(pair, axis=1) for pair in systems]
    for k in range(0, size, 2):
        done = []
        for wide in wides:
            first = jnp.broadcast_to(wide[:, k : k + 1], wide.shape)
            second = jnp.broadcast_to(wide[:, k + 1 : k + 2], wide.shape)
            a, c = first[k : k + 1], first[k + 1 : k + 2]
            b, d = second[k : k + 1], second[k + 1 : k + 2]
            one, two = wide[k : k + 1], wide[k + 1 : k + 2]
            inverse = 1.0 / (a * d - b * c)
            top = (d * one - b * two) * inverse
            low = (a * two - c * one) * inverse
            rest = wide - first * top - second * low
            done.append(jnp.where(row_ids == k, top, jnp.where(row_ids == k + 1, low, rest)))
        wides = done
    return [wide[:, size:] for wide in wides]


def identity(size):
    rows = lax.broadcasted_iota(jnp.int32, (size, size), 0)
    lanes = lax.broadcasted_iota(jnp.int32, (size, size), 1)
    return jnp.where(rows == lanes, 1.0, 0.0).astype(F32)


def coefficients(grams, previous):
    rhs = grams.shape[0]
    own_gram = grams[:, :rhs]
    image_gram = grams[:, rhs : 2 * rhs]
    if previous is None:
        return own_gram, image_gram, None
    old_inverse, old_gram = previous
    cross = grams[:, 2 * rhs : 3 * rhs]
    mix = dot_small(old_inverse, own_gram, 1)
    image_gram = image_gram + (
        dot_small(mix, cross, 0)
        + dot_small(cross, mix, 0)
        + dot_small(mix, dot_small(old_gram, mix, 1), 0)
    )
    return own_gram, image_gram, mix


def added(refs):
    total = refs[0][...]
    for ref in refs[1:]:
        total = total + ref[...]
    return total


def first_steps_kernel(*refs):
    step_ref, inverse_ref, gram_ref, minus_ref = refs[-4:]
    own_gram, image_gram, _ = coefficients(added(refs[:-4]), None)
    step, inverse = eliminate([(image_gram, own_gram), (own_gram, identity(own_gram.shape[0]))])
    step_ref[...] = step
    inverse_ref[...] = inverse
    gram_ref[...] = image_gram
    minus_ref[...] = -step


def next_steps_kernel(*refs):
    old_step_ref, old_inverse_ref, old_gram_ref = refs[-9:-6]
    step_ref, inverse_ref, gram_ref, mix_ref, base_ref, raw_ref = refs[-6:]
    previous = (old_inverse_ref[...], old_gram_ref[...])
    own_gram, image_gram, mix = coefficients(added(refs[:-9]), previous)
    step, inverse = eliminate([(image_gram, own_gram), (own_gram, identity(own_gram.shape[0]))])
    step_ref[...] = step
    inverse_ref[...] = inverse
    gram_ref[...] = image_gram
    mix_ref[...] = mix
    base_ref[...] = -step - dot_small(mix, step, 1)
    raw_ref[...] = dot_small(old_step_ref[...], step, 1)


def cost(flops, elements):
    return pl.CostEstimate(flops=flops, bytes_accessed=4 * elements, transcendentals=0)


def small_call(kernel, count, *operands):
    rhs = operands[0].shape[0]
    return pl.pallas_call(
        kernel,
        out_shape=[jax.ShapeDtypeStruct((rhs, rhs), F32)] * count,
        compiler_params=pltpu.CompilerParams(vmem_limit_bytes=2 * MIB),
        cost_estimate=cost(4 * 10**9, MIB),
    )(*operands)


def whole(ref):
    return jnp.concatenate([ref[j] for j in range(ref.shape[0])], axis=1)


def place(ref, value):
    tile = ref.shape[2]
    for j in range(ref.shape[0]):
        ref[j] = value[:, j * tile : (j + 1) * tile]


def gradient_kernel(g1_ref, q0_ref, p0_ref, step0_ref, step1_ref, mix_ref, g2_ref):
    q0 = whole(q0_ref)
    normal = q0 - dot_small(step0_ref[...], whole(p0_ref), 0) + dot_small(mix_ref[...], q0, 0)
    place(g2_ref, whole(g1_ref) - dot_small(step1_ref[...], normal, 0))


def next_gradient(*operands):
    return pl.pallas_call(
        gradient_kernel,
        out_shape=jax.ShapeDtypeStruct(operands[0].shape, F32),
        compiler_params=pltpu.CompilerParams(vmem_limit_bytes=4 * MIB),
        cost_estimate=cost(10**9, MIB),
    )(*operands)


def solution_kernel(g0_ref, g1_ref, step0_ref, step1_ref, mix_ref, direction_ref, sol_ref):
    g0 = whole(g0_ref)
    direction = whole(g1_ref) + dot_small(mix_ref[...], g0, 0)
    place(direction_ref, direction)
    sol_ref[...] = dot_small(step0_ref[...], g0, 0) + dot_small(step1_ref[...], direction, 0)


def solution_so_far(g0, *operands):
    row = jax.ShapeDtypeStruct((g0.shape[1], g0.shape[0] * g0.shape[2]), F32)
    return pl.pallas_call(
        solution_kernel,
        out_shape=[jax.ShapeDtypeStruct(g0.shape, F32), row],
        compiler_params=pltpu.CompilerParams(vmem_limit_bytes=4 * MIB),
        cost_estimate=cost(10**9, MIB),
    )(g0, *operands)


def images_kernel(y0_ref, y1_ref, u0_ref, mix_ref, base_ref, image_ref, next_ref):
    of_y0 = stack(mix_ref[...].T)
    of_u0 = stack(base_ref[...].T)
    width = 1024

    @pl.loop(0, y0_ref.shape[1] // width)
    def _(i):
        at = tile_at(i, width)
        y1 = y1_ref[:, at]
        image_ref[:, at] = y1 + combine(of_y0, *split(y0_ref[:, at]))
        next_ref[:, at] = y1 + combine(of_u0, *split(u0_ref[:, at]))


def images(y0, *operands):
    return pl.pallas_call(
        images_kernel,
        out_shape=[jax.ShapeDtypeStruct(y0.shape, F32)] * 2,
        compiler_params=pltpu.CompilerParams(vmem_limit_bytes=12 * MIB),
        cost_estimate=cost(3 * 10**9, MIB),
    )(y0, *operands)


def residual_kernel(y0_ref, image_ref, targets_ref, step0_ref, step1_ref, resid_ref):
    parts = stack(-jnp.concatenate([step0_ref[...], step1_ref[...]], axis=0).T)
    width = 1024

    @pl.loop(0, y0_ref.shape[1] // width)
    def _(i):
        at = tile_at(i, width)
        pair = jnp.concatenate([y0_ref[:, at], image_ref[:, at]], axis=0)
        resid_ref[:, at] = targets_ref[:, at] + combine(parts, *split(pair))


def residual_so_far(y0, *operands):
    return pl.pallas_call(
        residual_kernel,
        out_shape=jax.ShapeDtypeStruct(y0.shape, F32),
        compiler_params=pltpu.CompilerParams(vmem_limit_bytes=12 * MIB),
        cost_estimate=cost(2 * 10**9, 2 * MIB),
    )(y0, *operands)


def finish_kernel(*refs):
    *gram_refs, inverse_ref, gram_ref, resid_ref, image_ref, old_image_ref = refs[:-7]
    share_ref, old_ref, sol_ref, out_sol_ref, out_ref, new_ref, semaphores = refs[-7:]
    previous = (inverse_ref[...], gram_ref[...])
    own_gram, image_gram, mix = coefficients(added(gram_refs), previous)
    (step,) = eliminate([(image_gram, own_gram)])
    tile = share_ref.shape[2]
    both = jnp.concatenate([step, dot_small(mix, step, 1)], axis=0)
    pairs = [jnp.concatenate([share_ref[j], old_ref[j]], axis=0) for j in range(share_ref.shape[0])]
    out_sol_ref[...] = sol_ref[...] + dot_small(both, jnp.concatenate(pairs, axis=1), 0)
    minus = stack(-both.T)
    width = resid_ref.shape[1] // semaphores.shape[0]
    copies = []
    for i in range(semaphores.shape[0]):
        at = slice(i * width, (i + 1) * width)
        pair = jnp.concatenate([image_ref[:, at], old_image_ref[:, at]], axis=0)
        new_ref[:, at] = resid_ref[:, at] + combine(minus, *split(pair))
        copies.append(
            pltpu.make_async_copy(new_ref.at[:, at], out_ref.at[:, at], semaphores.at[i])
        )
        copies[-1].start()
    for copy in copies:
        copy.wait()


def finish(grams, previous, resid, image, old_image, share, old_share, sol):
    vmem = pl.BlockSpec(memory_space=pltpu.VMEM)
    return pl.pallas_call(
        finish_kernel,
        in_specs=[vmem] * (len(grams) + len(previous) + 6),
        out_specs=[vmem, pl.BlockSpec(memory_space=pl.ANY)],
        scratch_shapes=[pltpu.VMEM(resid.shape, F32), pltpu.SemaphoreType.DMA((4,))],
        out_shape=[
            jax.ShapeDtypeStruct(sol.shape, F32),
            jax.ShapeDtypeStruct(resid.shape, F32),
        ],
        compiler_params=pltpu.CompilerParams(vmem_limit_bytes=12 * MIB),
    )(*grams, *previous, resid, image, old_image, share, old_share, sol)


def mixed(small, wide):
    return jnp.einsum("mn,jmb->jnb", small, wide, precision=lax.Precision.HIGHEST)


def sum_kernel(starts, *refs):
    parts, outs = refs[: len(starts)], refs[len(starts) :]
    size = outs[0].shape[0] + len(outs) - 1
    total = parts[0][starts[0] : starts[0] + size]
    for start, part in zip(starts[1:], parts[1:]):
        total = total + part[start : start + size]
    if len(outs) == 1:
        outs[0][...] = total
    else:
        outs[0][...] = total[: size - 1]
        outs[1][...] = total[size - 1]


def sum_of(parts, size, apart=False):
    rest = parts[0][0].shape[1:]
    if apart:
        out_shape = [jax.ShapeDtypeStruct((size - 1,) + rest, F32), jax.ShapeDtypeStruct(rest, F32)]
    else:
        out_shape = [jax.ShapeDtypeStruct((size,) + rest, F32)]
    out = pl.pallas_call(
        functools.partial(sum_kernel, [start for _, start in parts]),
        out_shape=out_shape,
        compiler_params=pltpu.CompilerParams(vmem_limit_bytes=4 * MIB),
    )(*[array for array, _ in parts])
    return out if apart else out[0]


def sum_whole(parts):
    return sum_of([(part, 0) for part in parts], parts[0].shape[0])


def join_kernel(*refs):
    size = refs[0].shape[0]
    for i, part in enumerate(refs[: refs[-1].shape[0] // size]):
        refs[-1][i * size : (i + 1) * size] = part[...]


def join(parts, after):
    shape = parts[0].shape
    vmem = pl.BlockSpec(memory_space=pltpu.VMEM)
    return pl.pallas_call(
        join_kernel,
        in_specs=[vmem] * len(parts) + [pl.BlockSpec(memory_space=pl.ANY)] * len(after),
        out_specs=vmem,
        out_shape=jax.ShapeDtypeStruct((len(parts) * shape[0],) + shape[1:], F32),
        compiler_params=pltpu.CompilerParams(vmem_limit_bytes=4 * MIB),
    )(*parts, *after)


class Ring:
    def __init__(self, count):
        self.nz = 4 if count % 4 == 0 else count
        self.nx = count // self.nz
        self.order = [0] + list(range(1, self.nz, 2)) + list(range(2, self.nz, 2))[::-1]

    def row(self, place, x):
        return self.order[place % self.nz] * self.nx + x % self.nx

    def next_z(self, value, by=1):
        pairs = [
            (self.row(p, x), self.row(p + by, x)) for p in range(self.nz) for x in range(self.nx)
        ]
        return lax.ppermute(value, "row", pairs)

    def next_x(self, value):
        pairs = [
            (self.row(p, x), self.row(p, x + 1)) for p in range(self.nz) for x in range(self.nx)
        ]
        return lax.ppermute(value, "row", pairs)

    def place_of(self, row):
        z = row // self.nx
        return jnp.where(z % 2 == 1, (z + 1) // 2, (self.nz - z // 2) % self.nz)

    def slot_of(self, row):
        me = lax.axis_index("row")
        back_z = (self.place_of(me) - self.place_of(row) + self.nz) % self.nz
        back_x = (me % self.nx - row % self.nx + self.nx) % self.nx
        return back_z * self.nx + back_x

    def along_x(self, share):
        pieces = [share]
        for _ in range(1, self.nx):
            pieces.append(self.next_x(pieces[-1]))
        return pieces

    def gather(self, share, after=()):
        row = self.along_x(share)
        arrays = list(row)
        for _ in range(self.nz // 2):
            share = self.next_z(share)
            last = [share, arrays[-1], *after]
            arrays += self.along_x(share)
        back = []
        for _ in range((self.nz - 1) // 2):
            back.insert(0, self.next_z(back[0] if back else join(row, last), -1))
        return arrays + back

    def groups(self):
        back = (self.nz - 1) // 2
        return [1] * self.nx + [self.nx] * back + [1] * (self.nx * (self.nz - 1 - back))

    def scatter(self, arrays, apart=False):
        steps_back = (self.nz - 1) // 2
        size = arrays[0].shape[0]
        own, arrays = arrays[: self.nx], arrays[self.nx :]
        backs, arrays = arrays[:steps_back], arrays[steps_back:]

        def over_x(slots):
            parts = []
            for t in list(range(1, self.nx)) + [0]:
                if parts:
                    whole = len(parts) == 1 and parts[0][0].shape[0] == size
                    parts = [(self.next_x(parts[0][0] if whole else sum_of(parts, size)), 0)]
                parts = parts + slots[t]
            return parts

        ahead = []
        for f in range(self.nz // 2, 0, -1):
            at = (self.nz - f - 1 - steps_back) * self.nx
            piece = sum_of(over_x([[(arrays[at + t], 0)] for t in range(self.nx)]), size)
            ahead.append((self.next_z(piece, f), 0))
        back = [self.next_z(backs[s - 1], -s) for s in range(steps_back, 0, -1)]
        here = [
            [(own[t], 0)] + [(array, t * size) for array in back] for t in range(self.nx)
        ]
        return sum_of(over_x(here) + ahead, size, apart)


def exchanges(axes):
    steps = []
    for axis in axes:
        bits = (lax.axis_size(axis) - 1).bit_length()
        while bits:
            taken = 2 if bits > 1 else 1
            bits -= taken
            steps.append((axis, [flip << bits for flip in range(1, 1 << taken)]))
    return steps


def sum_over(value, axes):
    parts = [value]
    for at, (axis, flips) in enumerate(exchanges(axes)):
        if at:
            value = sum_whole(parts)
        parts = [value]
        for flip in flips:
            pairs = [(i, i ^ flip) for i in range(lax.axis_size(axis))]
            parts.append(lax.ppermute(value, axis, pairs))
    return parts


def body(blocks, block_cols, targets):
    row_count = lax.axis_size("row")
    col_count = lax.axis_size("col")
    ring = Ring(row_count)
    owner = block_cols // CBD // col_count
    cols = (ring.slot_of(owner) * CBD + block_cols % CBD).reshape(-1)

    groups = ring.groups()
    weights, *sums = prepare(cols, blocks, targets, groups)
    g0 = ring.scatter(sums)

    y0, *sums = sweep(cols, weights, ring.gather(g0), groups, g0, "first")
    q0, grams = ring.scatter(sums, True)
    grams = sum_over(grams, ("col",))
    step0, inverse, image_gram, minus = small_call(first_steps_kernel, 4, *grams)

    g1 = g0 + mixed(minus, q0)
    y1, u0, *sums = sweep(
        cols, weights, ring.gather(q0, [step0]), groups, g1, "middle", (y0, minus, y0)
    )
    p0, grams = ring.scatter(sums, True)
    grams = sum_over(grams, ("col",))
    step1, inverse, image_gram, mix, of_u0, of_raw = small_call(
        next_steps_kernel, 6, *grams, step0, inverse, image_gram
    )

    g2 = next_gradient(g1, q0, p0, step0, step1, mix)
    image, base = images(y0, y1, u0, mix, of_u0)
    y2, grams = sweep(
        cols, weights, ring.gather(p0), groups, g2, "last", (base, of_raw, image)
    )
    grams = sum_over(grams, ("col", "row"))
    direction, solution = solution_so_far(g0, g1, step0, step1, mix)
    residual = residual_so_far(y0, image, targets, step0, step1)
    return finish(
        grams, (inverse, image_gram), residual, y2, image, g2, direction, solution
    )


def solution(mesh):
    placed = (P(("row", "col"), None, None, None), P(("row", "col"), None), P(None, ("row", "col")))
    return jax.shard_map(
        body,
        mesh=mesh,
        in_specs=placed,
        out_specs=(P(None, ("row", "col")), P(None, ("row", "col"))),
        check_vma=False,
    )
```
